256 devices in a mesh: cand: 32 (over z, x_hi, core), query: 8 (over y, x_lo).
Axes of the slice: x: 4 (x_hi: 2, x_lo: 2; x = x_hi * 2 + x_lo), y: 4, z: 8, core: 2. Of those that a mesh axis runs over, the one named last changes fastest.
Arguments:
- pool: bfloat16 [327680, 4096], P(('cand', 'query')), may hold values from -6 to 6
- cand_ids: int32 [262144], P(('cand', 'query')), may hold values from 0 to 1279
- pick_ids: int32 [256], P(('cand', 'query')), may hold values from 0 to 1279
- queries: bfloat16 [1024, 4096], P('query'), may hold values from -6 to 6
Outputs:
- gains: float32 [262144], P(('cand', 'query'))
- coverage: float32 [1024], P('query')
The draws below stay inside these ranges and needn't reach their ends.
Inputs may be any that keep to these rules, and one draw needn't show every extreme that they name: `cand_ids`: each id is a row within the pool block of 1280 rows that lies on the same device as the id. `pick_ids`: each id is a row within the pool block of 1280 rows that lies on the same device as the id.
All inputs are finite; a program needn't handle non-finite values.
Results may differ from the reference program's by a relative error of at most 0.0003.
Values may be sent and summed in bfloat16 or wider, within the bound.
A program may use at most 128 MiB of HBM per device.

```python
import math
import jax
import jax.numpy as jnp
from jax import lax

D = 4096
CAND_DEV = 1024
PICK_DEV = 1
POOL_DEV = 1280
CANDS = 262144
PICKS = 256
POOL = 327680
Q = 1024


def set_ends(values, key, least, largest):
    shape = values.shape
    spot = [jax.random.randint(jax.random.fold_in(key, axis), (), 0, shape[axis]) for axis in range(len(shape))]
    values = values.at[tuple(spot)].set(least)
    longest = shape.index(max(shape))
    spot[longest] = (spot[longest] + 1) % shape[longest]
    return values.at[tuple(spot)].set(largest)


def level_of(rng, dims, shards, low, largest):
    level = 1.0
    for dim, shards_of in shards:
        draws = jax.random.uniform(jax.random.fold_in(jax.random.fold_in(rng, 6), dim), (shards_of,), jnp.float32, low / len(shards), largest / len(shards))
        level = level * jnp.repeat(jnp.exp(draws), dims[dim] // shards_of).reshape((-1,) + (1,) * (len(dims) - 1 - dim))
    return level


def scatter_about(key, dims, spread, limit, shards=(), kind=jnp.bfloat16):
    drawn = spread * jax.random.normal(key, dims, jnp.float32)
    if shards:
        drawn = drawn * level_of(key, dims, shards, -0.22, 0.18)
    return jnp.clip(drawn, -limit, limit).astype(kind)


def setup_inputs(seed: int = 0) -> dict:
    keys = jax.random.split(jax.random.key(seed), 5)
    pool = scatter_about(keys[0], (POOL, D), 1.0, 6.0, ((0, 256),))
    cand_ids = set_ends(jax.random.randint(keys[1], (CANDS,), 0, POOL_DEV), jax.random.fold_in(keys[1], 1), 0, POOL_DEV - 1).astype(jnp.int32)
    pick_ids = set_ends(jax.random.randint(keys[2], (PICKS,), 0, POOL_DEV), jax.random.fold_in(keys[2], 1), 0, POOL_DEV - 1).astype(jnp.int32)
    queries = scatter_about(keys[3], (Q, D), 1.0, 6.0, ((0, 8),))
    return dict(pool=pool, cand_ids=cand_ids, pick_ids=pick_ids, queries=queries)


def similarity(rows, targets):
    product = lax.dot_general(rows, targets, (((1,), (1,)), ((), ())), preferred_element_type=jnp.float32)
    return product * (1.0 / math.sqrt(D))

def reference(pool, cand_ids, pick_ids, queries):
    blocks = pool.shape[0] // POOL_DEV
    pool_blocks = pool.reshape(blocks, POOL_DEV, D)
    cand_blocks = cand_ids.reshape(blocks, CAND_DEV)
    pick_blocks = pick_ids.reshape(blocks, PICK_DEV)

    def pick_best(args):
        rows, ids = args
        return lax.optimization_barrier(jnp.max(similarity(rows[ids], queries), axis=0))
    coverage = lax.optimization_barrier(jnp.max(lax.map(pick_best, (pool_blocks, pick_blocks)), axis=0))

    def cand_gain(args):
        rows, ids = args
        scores = similarity(rows[ids], queries)
        gained = lax.optimization_barrier(jnp.sum(jnp.maximum(scores - coverage[None, :], 0.0), axis=1))
        return gained + 1.0 * lax.optimization_barrier(jnp.max(scores, axis=1))
    gains = lax.map(cand_gain, (pool_blocks, cand_blocks)).reshape(-1)
    return (gains, coverage)
```

```python
import jax
import jax.numpy as jnp
from jax import lax
from jax.experimental import pallas as pl
from jax.experimental.pallas import tpu as pltpu
from jax.sharding import PartitionSpec as P

MESH = pl.DeviceIdType.MESH
D = 4096
TILE = 128
BLOCK = 128
POOL = 1280
SCALE = 1.0 / 64.0
OWN, X, YP, YM, XP, XM, Y2, X2 = range(8)
DELTA = {X: (0, 1), YP: (1, 0), YM: (3, 0), XP: (1, 1), XM: (3, 1), Y2: (2, 0), X2: (2, 1)}


def where_am_i():
    cand, query = lax.axis_index("cand"), lax.axis_index("query")
    core = lax.rem(cand, 2)
    x = lax.rem(lax.div(cand, 2), 2) * 2 + lax.rem(query, 2)
    return x, lax.div(query, 2), lax.div(cand, 4), core


def device(x, y, z, core):
    return ((z * 2 + lax.div(x, 2)) * 2 + core, y * 2 + lax.rem(x, 2))


def dot(a, b):
    return lax.dot_general(a, b, (((1,), (1,)), ((), ())), preferred_element_type=jnp.float32)


def gather_and_score(
    pick_ref, pool_ref, q_ref, part_ref, cover_ref,
    allq, pool, scores, pick_f32, pick_buf, pick_rows, cover_x, cover_z, cover_q, columns,
    local_sem, send_sem, recv_sem,
):
    x, y, z, core = where_am_i()
    odd = lax.rem(z, 2)
    x_pair = x + 1 - 2 * lax.rem(x, 2)

    def step(v, by, size):
        return lax.rem(v + by + size, size)

    target = {
        "x+": device(step(x, 1, 4), y, z, core),
        "x-": device(step(x, -1, 4), y, z, core),
        "y+": device(x, step(y, 1, 4), z, core),
        "y-": device(x, step(y, -1, 4), z, core),
        "z+": device(x, y, step(z, 1, 8), core),
        "z-": device(x, y, step(z, -1, 8), core),
        "s": device(x, y, z, 1 - core),
    }
    query_group = {
        b: device(x_pair if dx else x, step(y, dy, 4), z, core) for b, (dy, dx) in DELTA.items()
    }
    x_far = step(x, 2, 4)
    four = [device(x_far, y, z, core), device(x, y, z, 1 - core), device(x_far, y, z, 1 - core)]
    column_group = [device(x, y, step(z, d, 8), core) for d in range(1, 8)]

    half_pool = POOL // 2
    pool_copies = [
        pltpu.make_async_copy(
            pool_ref.at[pl.ds(h * half_pool, half_pool)],
            pool.at[pl.ds(h * half_pool, half_pool)],
            local_sem.at[h],
        )
        for h in range(2)
    ]
    own_copy = pltpu.make_async_copy(q_ref, allq.at[pl.ds(0, BLOCK)], local_sem.at[2])
    own_copy.start()
    for c in pool_copies:
        c.start()

    barrier = pltpu.get_barrier_semaphore()
    partners = list(query_group.values()) + four + column_group
    partners += [device(lax.rem(x_pair + 2, 4), y, z, core)]
    for p in partners:
        pl.semaphore_signal(barrier, inc=1, device_id=p, device_id_type=MESH)
    pl.semaphore_wait(barrier, len(partners))

    def pick_col(if_odd, if_even):
        return pl.multiple_of((if_even + odd * (if_odd - if_even)) * TILE, TILE)

    IN = {
        "0": (0, 28, 4), "1": (4, 24, 4), "2": (8, 20, 4), "3": (12, 16, 4), "4": (16, 12, 4),
        "4a": (16, 12, 2), "4b": (18, 14, 2), "01": (0, 24, 8), "23": (8, 16, 8), "012": (0, 20, 12),
        "E": (0, 16, 16), "L": (16, 0, 16),
        "z0": (28, 0, 4), "z1": (24, 4, 4), "z2": (20, 8, 4),
    }

    copies = {}
    made = []

    def send(name, to, src_block, dst_block, cols, rows=(0, 64)):
        if_odd, if_even, tiles = IN[cols]
        width = pl.ds(pick_col(if_odd, if_even), tiles * TILE)
        first = pl.multiple_of(core * 64 + rows[0], 32)
        src = q_ref if src_block == OWN else allq
        n = len(made)
        c = pltpu.make_async_remote_copy(
            src_ref=src.at[pl.ds(pl.multiple_of(src_block * BLOCK + first, 32), rows[1]), width],
            dst_ref=allq.at[pl.ds(pl.multiple_of(dst_block * BLOCK + first, 32), rows[1]), width],
            send_sem=send_sem.at[n],
            recv_sem=recv_sem.at[n],
            device_id=target[to],
            device_id_type=MESH,
        )
        made.append(c)
        copies[name] = c
        c.start()

    def send_small(name, src, dst, to):
        n = len(made)
        c = pltpu.make_async_remote_copy(
            src_ref=src, dst_ref=dst, send_sem=send_sem.at[n], recv_sem=recv_sem.at[n],
            device_id=to, device_id_type=MESH,
        )
        made.append(c)
        copies[name] = c
        c.start()

    def got(*names):
        for name in names:
            copies.pop(name).wait_recv()

    def along_z(block, cols):
        send(f"z+{block}{cols}", "z+", block, block, cols, (0, 32))
        send(f"z-{block}{cols}", "z-", block, block, cols, (32, 32))

    def got_z(block, *cols):
        for c in cols:
            got(f"z+{block}{c}", f"z-{block}{c}")

    def share(block, part):
        send(f"s{block}{part}", "s", block, block, part)

    def got_share(block, part):
        got(f"s{block}{part}")

    def score(pair, part):
        if_odd, if_even, tiles = IN[part]
        width = pl.ds(pick_col(if_odd, if_even), tiles * TILE)
        rows = pl.ds(pair * 2 * BLOCK, 2 * BLOCK)
        s = dot(allq[rows, width], pool[:, width])
        if part == "E":
            scores[rows, :] = s
        else:
            scores[rows, :] = scores[rows, :] + s

    send("YP0", "y-", OWN, YP, "0")
    send("YM0", "y+", OWN, YM, "0")
    send("X01", "x+", OWN, X, "01")
    send("X23", "x-", OWN, X, "23")
    send("YP1", "y-", OWN, YP, "1")
    send("YM1", "y+", OWN, YM, "1")
    send("X4a", "x+", OWN, X, "4a")
    send("X4b", "x-", OWN, X, "4b")
    for k in "234":
        send("YP" + k, "y-", OWN, YP, k)
        send("YM" + k, "y+", OWN, YM, k)

    def onward(k):
        got("YP" + k, "YM" + k)
        send("XP" + k, "x+", YP, XP, k)
        send("XM" + k, "x-", YM, XM, k)

    onward("0")

    for c in pool_copies:
        c.wait()
    pick = pick_ref[0]
    near = pool.reshape(POOL // 16, 16, D)[lax.div(pick, 16)].astype(jnp.float32)
    is_pick = lax.broadcasted_iota(jnp.int32, (16, D), 0) == lax.rem(pick, 16)
    row = jnp.sum(jnp.where(is_pick, near, 0.0), axis=0, keepdims=True)
    for i in range(D // TILE):
        pick_f32[pl.ds(i, 1), :] = row[:, i * TILE : (i + 1) * TILE]
    pick_buf[pl.ds(0, 32), :] = pick_f32[pl.ds(0, 32), :].astype(jnp.bfloat16)
    back = {X: X, YP: YM, YM: YP, XP: XM, XM: XP, Y2: Y2, X2: X2}
    for b, to in query_group.items():
        send_small(f"p{b}", pick_buf.at[pl.ds(0, 32)], pick_buf.at[pl.ds(back[b] * 32, 32)], to)

    got("X01", "X23")
    share(X, "E")
    along_z(X, "01")
    along_z(X, "2")
    onward("1")
    along_z(YP, "01")
    along_z(YM, "01")
    onward("2")
    along_z(YP, "2")
    along_z(YM, "2")

    own_copy.wait()
    got(*[f"p{b}" for b in query_group])
    pick_f32[...] = pick_buf[...].astype(jnp.float32)
    for i in range(D // TILE):
        pick_rows[:, pl.ds(i * TILE, TILE)] = pick_f32[pl.ds(i, 8, stride=32), :]
    eight = pick_rows[...].astype(jnp.bfloat16)
    sims = dot(jnp.concatenate([eight, eight], axis=0), allq[pl.ds(0, BLOCK), :])
    best = jnp.broadcast_to(jnp.max(sims, axis=0, keepdims=True), (8, TILE))
    cover_x[pl.ds(0, 8), :] = best
    for i, to in enumerate(four):
        send_small(f"cx{i}", cover_x.at[pl.ds(0, 8)], cover_x.at[pl.ds(8 + 8 * i, 8)], to)

    got_share(X, "E")
    score(0, "E")

    onward("3")
    send("Y2a", "y-", YP, Y2, "01")
    send("Y2b", "y+", YM, Y2, "23")
    share(YP, "E")
    share(YM, "E")
    onward("4")
    send("Y2c", "y-", YP, Y2, "4a")
    send("Y2d", "y+", YM, Y2, "4b")

    got("cx0", "cx1", "cx2")
    best = jnp.maximum(
        jnp.maximum(cover_x[pl.ds(0, 8), :], cover_x[pl.ds(8, 8), :]),
        jnp.maximum(cover_x[pl.ds(16, 8), :], cover_x[pl.ds(24, 8), :]),
    )
    cover_z[pl.ds(0, 8), :] = best
    for i, to in enumerate(column_group):
        send_small(f"cz{i}", cover_z.at[pl.ds(0, 8)], cover_z.at[pl.ds(8 + 8 * i, 8)], to)

    got("XP0", "XM0", "XP1", "XM1")
    got("X4a", "X4b")
    got_z(X, "01", "2")
    share(X, "L")
    got_share(YP, "E")
    got_share(YM, "E")
    score(1, "E")
    got("XP2", "XM2")
    along_z(XP, "012")
    along_z(XM, "012")
    got("Y2a", "Y2b")
    send("X2a", "x+", Y2, X2, "0")
    send("X2b", "x-", Y2, X2, "2")
    send("X2c", "y-", XP, X2, "1")
    along_z(Y2, "012")
    share(Y2, "E")
    got_z(YP, "01", "2")
    got_z(YM, "01", "2")
    share(YP, "L")
    share(YM, "L")
    got_share(X, "L")
    score(0, "L")
    got("XP3", "XM3")
    send("X2d", "y+", XM, X2, "3")
    share(XP, "E")
    share(XM, "E")

    got(*[f"cz{i}" for i in range(7)])
    best = cover_z[pl.ds(0, 8), :]
    for i in range(7):
        best = jnp.maximum(best, cover_z[pl.ds(8 + 8 * i, 8), :])
    cover_q[pl.ds(0, 8), :] = best
    cover_ref[...] = best
    for b, to in query_group.items():
        send_small(f"cq{b}", cover_q.at[pl.ds(0, 8)], cover_q.at[pl.ds(back[b] * 8, 8)], to)

    got("XP4", "XM4", "Y2c", "Y2d")
    got_share(YP, "L")
    got_share(YM, "L")
    score(1, "L")
    got_z(Y2, "012")
    send("X2e", "x+", Y2, X2, "z0")
    send("X2f", "x-", Y2, X2, "z1")
    share(Y2, "L")
    got_z(XP, "012")
    got_z(XM, "012")
    send("X2g", "y-", XP, X2, "z2")
    send("X2h", "y+", XM, X2, "4")
    share(XP, "L")
    share(XM, "L")
    got_share(XP, "E")
    got_share(XM, "E")
    score(2, "E")
    got("X2a", "X2b", "X2c", "X2d")
    share(X2, "E")
    got_share(XP, "L")
    got_share(XM, "L")
    score(2, "L")
    got("X2e", "X2f", "X2g", "X2h")
    share(X2, "L")
    got_share(Y2, "E")
    got_share(X2, "E")
    score(3, "E")

    got(*[f"cq{b}" for b in query_group])
    rows = jnp.concatenate(
        [cover_q[pl.ds(8 * b, 1), :] for b in range(8)] + [jnp.zeros((TILE - 8, TILE), jnp.float32)], axis=0
    )
    turned = rows.T
    for b in range(8):
        columns[pl.ds(b * BLOCK, BLOCK), :] = jnp.broadcast_to(turned[:, b : b + 1], (BLOCK, TILE))

    def gain(first, groups, carry):
        def body(g, carry):
            summed, highest = carry
            r = pl.ds(pl.multiple_of(first + g * 8, 8), 8)
            s = scores[r, :]
            c = jnp.concatenate([columns[r, :]] * (POOL // TILE), axis=1)
            return summed + jnp.maximum(s - c, 0.0), jnp.maximum(highest, s)

        return lax.fori_loop(0, groups, body, carry)

    start = (jnp.zeros((8, POOL), jnp.float32), jnp.full((8, POOL), -jnp.inf, jnp.float32))
    carry = gain(0, 6 * BLOCK // 8, start)
    part_ref[pl.ds(0, 8), :] = carry[0]
    part_ref[pl.ds(8, 8), :] = carry[1]
    got_share(Y2, "L")
    got_share(X2, "L")
    score(3, "L")
    carry = gain(6 * BLOCK, 2 * BLOCK // 8, (part_ref[pl.ds(0, 8), :], part_ref[pl.ds(8, 8), :]))
    part_ref[pl.ds(0, 8), :] = carry[0]
    part_ref[pl.ds(8, 8), :] = carry[1]
    for c in made:
        c.wait_send()


COPIES = 100


def choose(part_ref, cover_ref, ids_ref, gains_ref, out_cover_ref):
    summed = jnp.sum(part_ref[pl.ds(0, 8), :], axis=0, keepdims=True)
    highest = jnp.max(part_ref[pl.ds(8, 8), :], axis=0, keepdims=True)
    gain = summed * SCALE + 1.0 * (highest * SCALE)
    ids = ids_ref[...]
    lane, group = jnp.bitwise_and(ids, TILE - 1), jnp.right_shift(ids, 7)
    out = jnp.zeros(ids.shape, jnp.float32)
    for k in range(POOL // TILE):
        row = jnp.broadcast_to(gain[:, k * TILE : (k + 1) * TILE], ids.shape)
        out = jnp.where(group == k, jnp.take_along_axis(row, lane, axis=1, mode="promise_in_bounds"), out)
    gains_ref[...] = out
    out_cover_ref[...] = cover_ref[pl.ds(0, 1), :] * SCALE


def on_device(pool, cand_ids, pick_ids, queries):
    f32, bf16 = jnp.float32, jnp.bfloat16
    vmem = pl.BlockSpec(memory_space=pltpu.VMEM)
    part, cover = pl.pallas_call(
        gather_and_score,
        name="gather_and_score",
        out_shape=(jax.ShapeDtypeStruct((16, POOL), f32), jax.ShapeDtypeStruct((8, TILE), f32)),
        in_specs=[
            pl.BlockSpec(memory_space=pltpu.SMEM),
            pl.BlockSpec(memory_space=pl.ANY),
            pl.BlockSpec(memory_space=pl.ANY),
        ],
        out_specs=(vmem, vmem),
        scratch_shapes=[
            pltpu.VMEM((8 * BLOCK, D), bf16),
            pltpu.VMEM((POOL, D), bf16),
            pltpu.VMEM((8 * BLOCK, POOL), f32),
            pltpu.VMEM((256, TILE), f32),
            pltpu.VMEM((256, TILE), bf16),
            pltpu.VMEM((8, D), f32),
            pltpu.VMEM((32, TILE), f32),
            pltpu.VMEM((64, TILE), f32),
            pltpu.VMEM((64, TILE), f32),
            pltpu.VMEM((8 * BLOCK, TILE), f32),
            pltpu.SemaphoreType.DMA((3,)),
            pltpu.SemaphoreType.DMA((COPIES,)),
            pltpu.SemaphoreType.DMA((COPIES,)),
        ],
        compiler_params=pltpu.CompilerParams(
            collective_id=0, has_side_effects=True, vmem_limit_bytes=60 << 20
        ),
        cost_estimate=pl.CostEstimate(
            flops=2 * POOL * 1024 * D, bytes_accessed=POOL * D * 2, transcendentals=0
        ),
    )(pick_ids, pool, queries)
    gains, own_cover = pl.pallas_call(
        choose,
        name="choose",
        out_shape=(jax.ShapeDtypeStruct((8, TILE), f32), jax.ShapeDtypeStruct((1, TILE), f32)),
        in_specs=[vmem, vmem, vmem],
        out_specs=(vmem, vmem),
    )(part, cover, cand_ids.reshape(8, TILE))
    return gains.reshape(-1), own_cover.reshape(-1)


def solution(mesh):
    in_specs = (
        P(("cand", "query"), None),
        P(("cand", "query")),
        P(("cand", "query")),
        P("query", None),
    )
    out_specs = (P(("cand", "query")), P("query"))
    return jax.shard_map(
        on_device, mesh=mesh, in_specs=in_specs, out_specs=out_specs, check_vma=False
    )
```

```python
import jax
import jax.numpy as jnp
from jax import lax
from jax.experimental import pallas as pl
from jax.experimental.pallas import tpu as pltpu
from jax.sharding import PartitionSpec as P

MESH = pl.DeviceIdType.MESH
D = 4096
TILE = 128
BLOCK = 128
POOL = 1280
SCALE = 1.0 / 64.0
SMALL = ["", "p", "cx", "cz", "cq"]
OWN, X, YP, YM, XP, XM, Y2, X2 = range(8)
DELTA = {X: (0, 1), YP: (1, 0), YM: (3, 0), XP: (1, 1), XM: (3, 1), Y2: (2, 0), X2: (2, 1)}


def where_am_i():
    cand, query = lax.axis_index("cand"), lax.axis_index("query")
    core = lax.rem(cand, 2)
    x = lax.rem(lax.div(cand, 2), 2) * 2 + lax.rem(query, 2)
    return x, lax.div(query, 2), lax.div(cand, 4), core


def device(x, y, z, core):
    return ((z * 2 + lax.div(x, 2)) * 2 + core, y * 2 + lax.rem(x, 2))


def dot(a, b):
    return lax.dot_general(a, b, (((1,), (1,)), ((), ())), preferred_element_type=jnp.float32)


def gather_and_score(
    pick_ref, pool_ref, q_ref, part_ref, cover_ref,
    allq, pool, scores, pick_f32, pick_buf, pick_rows, cover_x, cover_z, cover_q, columns,
    local_sem, send_sem, recv_sem,
):
    x, y, z, core = where_am_i()
    odd = lax.rem(z, 2)
    x_pair = x + 1 - 2 * lax.rem(x, 2)

    def step(v, by, size):
        return lax.rem(v + by + size, size)

    target = {
        "x+": device(step(x, 1, 4), y, z, core),
        "x-": device(step(x, -1, 4), y, z, core),
        "y+": device(x, step(y, 1, 4), z, core),
        "y-": device(x, step(y, -1, 4), z, core),
        "z+": device(x, y, step(z, 1, 8), core),
        "z-": device(x, y, step(z, -1, 8), core),
        "s": device(x, y, z, 1 - core),
    }
    query_group = {
        b: device(x_pair if dx else x, step(y, dy, 4), z, core) for b, (dy, dx) in DELTA.items()
    }
    x_far = step(x, 2, 4)
    four = [device(x_far, y, z, core), device(x, y, z, 1 - core), device(x_far, y, z, 1 - core)]
    column_group = [device(x, y, step(z, d, 8), core) for d in range(1, 8)]

    half_pool = POOL // 2
    pool_copies = [
        pltpu.make_async_copy(
            pool_ref.at[pl.ds(h * half_pool, half_pool)],
            pool.at[pl.ds(h * half_pool, half_pool)],
            local_sem.at[h],
        )
        for h in range(2)
    ]
    own_copy = pltpu.make_async_copy(q_ref, allq.at[pl.ds(0, BLOCK)], local_sem.at[2])
    own_copy.start()
    for c in pool_copies:
        c.start()

    barrier = pltpu.get_barrier_semaphore()
    partners = list(query_group.values()) + four + column_group
    partners += [device(lax.rem(x_pair + 2, 4), y, z, core)]
    for p in partners:
        pl.semaphore_signal(barrier, inc=1, device_id=p, device_id_type=MESH)
    pl.semaphore_wait(barrier, len(partners))

    def pick_col(if_odd, if_even):
        return pl.multiple_of((if_even + odd * (if_odd - if_even)) * TILE, TILE)

    COLS = {
        "c0": (0, 24, 8), "c1": (8, 16, 8), "c2": (16, 8, 8), "cz": (24, 0, 8),
        "c2a": (16, 8, 4), "c2b": (20, 12, 4), "cza": (24, 0, 4), "czb": (28, 4, 4), "e": (0, 16, 16), "l": (16, 0, 16), "all": (0, 0, 32),
    }

    groups = {}
    sent = [0]

    def send(group, to, src_block, dst_block, cols, rows=(0, 64)):
        if_odd, if_even, tiles = COLS[cols]
        width = pl.ds(pick_col(if_odd, if_even), tiles * TILE)
        first = pl.multiple_of(core * 64 + rows[0], 32)
        src = q_ref if src_block == OWN else allq
        n = groups.setdefault(group, [len(groups), 0, tiles])
        n[1] += rows[1]
        sent[0] += rows[1] // 32 * tiles
        pltpu.make_async_remote_copy(
            src_ref=src.at[pl.ds(pl.multiple_of(src_block * BLOCK + first, 32), rows[1]), width],
            dst_ref=allq.at[pl.ds(pl.multiple_of(dst_block * BLOCK + first, 32), rows[1]), width],
            send_sem=send_sem.at[0],
            recv_sem=recv_sem.at[n[0]],
            device_id=target[to],
            device_id_type=MESH,
        ).start()

    def send_small(group, src, dst, to):
        n = groups.setdefault(group, [len(groups), 0, 1])
        pltpu.make_async_remote_copy(
            src_ref=src, dst_ref=dst, send_sem=send_sem.at[SMALL.index(group)], recv_sem=recv_sem.at[n[0]],
            device_id=to, device_id_type=MESH,
        ).start()

    def got(*names):
        for group in names:
            n, rows, tiles = groups[group]
            ref = allq.at[pl.ds(0, rows), pl.ds(0, tiles * TILE)]
            pltpu.make_async_copy(ref, ref, recv_sem.at[n]).wait()

    def all_small(group, ref, rows):
        ref = ref.at[pl.ds(0, rows)]
        return pltpu.make_async_copy(ref, ref, recv_sem.at[groups[group][0]])

    def along_z(group, block, cols):
        send(group, "z+", block, block, cols, (0, 32))
        send(group, "z-", block, block, cols, (32, 32))

    def share(group, part, *blocks):
        for block in blocks:
            send(group, "s", block, block, part)

    def score(step):
        rows = pl.ds(pl.multiple_of((2 * lax.div(step, 4) + lax.rem(step, 2)) * 2 * BLOCK, 2 * BLOCK), 2 * BLOCK)
        late = lax.div(lax.rem(step, 4), 2)
        width = pl.ds(pl.multiple_of(lax.rem(late + 1 + odd, 2) * (D // 2), D // 2), D // 2)
        scores[rows, :] = scores[rows, :] + dot(allq[rows, width], pool[:, width])

    def gain(first, groups, carry):
        def body(g, carry):
            summed, highest = carry
            r = pl.ds(pl.multiple_of(first + g * 8, 8), 8)
            s = scores[r, :]
            c = jnp.concatenate([columns[r, :]] * (POOL // TILE), axis=1)
            return summed + jnp.maximum(s - c, 0.0), jnp.maximum(highest, s)

        return lax.fori_loop(0, groups, body, carry)

    send("Y0", "y-", OWN, YP, "c0")
    send("Y0", "y+", OWN, YM, "c0")
    send("X", "x+", OWN, X, "c0")
    send("X", "x-", OWN, X, "c1")

    own_copy.wait()
    for c in pool_copies:
        c.wait()
    pick = pick_ref[0]
    near = pool.reshape(POOL // 16, 16, D)[lax.div(pick, 16)].astype(jnp.float32)
    is_pick = lax.broadcasted_iota(jnp.int32, (16, D), 0) == lax.rem(pick, 16)
    row = jnp.sum(jnp.where(is_pick, near, 0.0), axis=0, keepdims=True)
    for i in range(D // TILE):
        pick_f32[pl.ds(i, 1), :] = row[:, i * TILE : (i + 1) * TILE]
    pick_buf[pl.ds(0, 32), :] = pick_f32[pl.ds(0, 32), :].astype(jnp.bfloat16)
    back = {X: X, YP: YM, YM: YP, XP: XM, XM: XP, Y2: Y2, X2: X2}
    for b, to in query_group.items():
        send_small("p", pick_buf.at[pl.ds(0, 32)], pick_buf.at[pl.ds(back[b] * 32, 32)], to)

    for k in "12":
        send("Y" + k, "y-", OWN, YP, "c" + k)
        send("Y" + k, "y+", OWN, YM, "c" + k)

    def clear(g, _):
        scores[pl.ds(pl.multiple_of(g * 8, 8), 8), :] = jnp.zeros((8, POOL), jnp.float32)
        return 0

    lax.fori_loop(0, 8 * BLOCK // 8, clear, 0)

    def before_0():
        got("Y0")
        send("XP0", "x+", YP, XP, "c0")
        send("XP0", "x-", YM, XM, "c0")
        along_z("zY", YP, "c0")
        along_z("zY", YM, "c0")
        got("X")
        share("sXe", "e", X)
        along_z("zX", X, "e")
        all_small("p", pick_buf, 7 * 32).wait()
        pick_f32[...] = pick_buf[...].astype(jnp.float32)
        for i in range(D // TILE):
            pick_rows[:, pl.ds(i * TILE, TILE)] = pick_f32[pl.ds(i, 8, stride=32), :]
        eight = pick_rows[...].astype(jnp.bfloat16)
        sims = dot(jnp.concatenate([eight, eight], axis=0), allq[pl.ds(0, BLOCK), :])
        cover_x[pl.ds(0, 8), :] = jnp.broadcast_to(jnp.max(sims, axis=0, keepdims=True), (8, TILE))
        for i, to in enumerate(four):
            send_small("cx", cover_x.at[pl.ds(0, 8)], cover_x.at[pl.ds(8 + 8 * i, 8)], to)
        got("Y1")
        send("XP1", "x+", YP, XP, "c1")
        send("XP1", "x-", YM, XM, "c1")
        share("sYe", "e", YP, YM)
        send("Y2e", "y-", YP, Y2, "c0")
        send("Y2e", "y+", YM, Y2, "c1")
        got("sXe")

    def before_1():
        got("zY")
        send("XPz", "x+", YP, XP, "cz")
        send("XPz", "x-", YM, XM, "cz")
        got("Y2")
        send("XP2", "x+", YP, XP, "c2")
        send("XP2", "x-", YM, XM, "c2")
        send("Y2l", "y-", YP, Y2, "cz")
        send("Y2l", "y+", YM, Y2, "c2")
        share("sYl", "l", YP, YM)
        got("zX")
        share("sXl", "l", X)
        got("sYe")

    def before_2():
        got("XP0", "XP1")
        send("X2e", "y-", XP, X2, "c0")
        send("X2e", "y+", XM, X2, "c1")
        share("sXPe", "e", XP, XM)
        got("Y2e")
        share("sY2e", "e", Y2)
        all_small("cx", cover_x, 24).wait()
        best = jnp.maximum(
            jnp.maximum(cover_x[pl.ds(0, 8), :], cover_x[pl.ds(8, 8), :]),
            jnp.maximum(cover_x[pl.ds(16, 8), :], cover_x[pl.ds(24, 8), :]),
        )
        cover_z[pl.ds(0, 8), :] = best
        for i, to in enumerate(column_group):
            send_small("cz", cover_z.at[pl.ds(0, 8)], cover_z.at[pl.ds(8 + 8 * i, 8)], to)
        got("sXl")

    def before_3():
        got("sYl")

    def before_4():
        got("Y2l")
        send("X2l", "x+", Y2, X2, "c2a")
        send("X2l", "x-", Y2, X2, "c2b")
        got("XPz")
        send("X2l", "y-", XP, X2, "cza")
        send("X2l", "y+", XM, X2, "czb")
        share("sY2l", "l", Y2)
        got("sXPe")

    def before_5():
        all_small("cz", cover_z, 56).wait()
        best = cover_z[pl.ds(0, 8), :]
        for i in range(7):
            best = jnp.maximum(best, cover_z[pl.ds(8 + 8 * i, 8), :])
        cover_q[pl.ds(0, 8), :] = best
        cover_ref[...] = best
        for b, to in query_group.items():
            send_small("cq", cover_q.at[pl.ds(0, 8)], cover_q.at[pl.ds(back[b] * 8, 8)], to)
        got("XP2")
        share("sXPl", "l", XP, XM)
        got("X2e")
        share("sX2e", "e", X2)
        got("sY2e", "sX2e")

    def before_6():
        got("X2l")
        share("sX2l", "l", X2)
        got("sXPl")

    def before_7():
        all_small("cq", cover_q, 56).wait()
        rows = jnp.concatenate(
            [cover_q[pl.ds(8 * b, 1), :] for b in range(8)] + [jnp.zeros((TILE - 8, TILE), jnp.float32)], axis=0
        )
        turned = rows.T
        for b in range(8):
            columns[pl.ds(b * BLOCK, BLOCK), :] = jnp.broadcast_to(turned[:, b : b + 1], (BLOCK, TILE))
        start = (jnp.zeros((8, POOL), jnp.float32), jnp.full((8, POOL), -jnp.inf, jnp.float32))
        summed, highest = gain(0, 6 * BLOCK // 8, start)
        part_ref[pl.ds(0, 8), :] = summed
        part_ref[pl.ds(8, 8), :] = highest
        got("sY2l", "sX2l")

    before = [before_0, before_1, before_2, before_3, before_4, before_5, before_6, before_7]

    def one_step(step, _):
        for k, segment in enumerate(before):
            pl.when(step == k)(segment)
        score(step)
        return 0

    lax.fori_loop(0, len(before), one_step, 0)

    summed, highest = gain(6 * BLOCK, 2 * BLOCK // 8, (part_ref[pl.ds(0, 8), :], part_ref[pl.ds(8, 8), :]))
    part_ref[pl.ds(0, 8), :] = summed
    part_ref[pl.ds(8, 8), :] = highest

    wide, rest = divmod(sent[0], 8 * BLOCK // 32)
    for n, tiles in ((8 * BLOCK, wide), (rest * 32, 1)):
        if n and tiles:
            ref = allq.at[pl.ds(0, n), pl.ds(0, tiles * TILE)]
            pltpu.make_async_copy(ref, ref, send_sem.at[0]).wait()
    for group, buffer, rows in (("p", pick_buf, 224), ("cx", cover_x, 24), ("cz", cover_z, 56), ("cq", cover_q, 56)):
        ref = buffer.at[pl.ds(0, rows)]
        pltpu.make_async_copy(ref, ref, send_sem.at[SMALL.index(group)]).wait()


def choose(part_ref, cover_ref, ids_ref, gains_ref, out_cover_ref):
    summed = jnp.sum(part_ref[pl.ds(0, 8), :], axis=0, keepdims=True)
    highest = jnp.max(part_ref[pl.ds(8, 8), :], axis=0, keepdims=True)
    gain = summed * SCALE + 1.0 * (highest * SCALE)
    ids = ids_ref[...]
    lane, group = jnp.bitwise_and(ids, TILE - 1), jnp.right_shift(ids, 7)
    out = jnp.zeros(ids.shape, jnp.float32)
    for k in range(POOL // TILE):
        row = jnp.broadcast_to(gain[:, k * TILE : (k + 1) * TILE], ids.shape)
        out = jnp.where(group == k, jnp.take_along_axis(row, lane, axis=1, mode="promise_in_bounds"), out)
    gains_ref[...] = out
    out_cover_ref[...] = cover_ref[pl.ds(0, 1), :] * SCALE


def on_device(pool, cand_ids, pick_ids, queries):
    f32, bf16 = jnp.float32, jnp.bfloat16
    vmem = pl.BlockSpec(memory_space=pltpu.VMEM)
    part, cover = pl.pallas_call(
        gather_and_score,
        name="gather_and_score",
        out_shape=(jax.ShapeDtypeStruct((16, POOL), f32), jax.ShapeDtypeStruct((8, TILE), f32)),
        in_specs=[
            pl.BlockSpec(memory_space=pltpu.SMEM),
            pl.BlockSpec(memory_space=pl.ANY),
            pl.BlockSpec(memory_space=pl.ANY),
        ],
        out_specs=(vmem, vmem),
        scratch_shapes=[
            pltpu.VMEM((8 * BLOCK, D), bf16),
            pltpu.VMEM((POOL, D), bf16),
            pltpu.VMEM((8 * BLOCK, POOL), f32),
            pltpu.VMEM((256, TILE), f32),
            pltpu.VMEM((256, TILE), bf16),
            pltpu.VMEM((8, D), f32),
            pltpu.VMEM((32, TILE), f32),
            pltpu.VMEM((64, TILE), f32),
            pltpu.VMEM((64, TILE), f32),
            pltpu.VMEM((8 * BLOCK, TILE), f32),
            pltpu.SemaphoreType.DMA((3,)),
            pltpu.SemaphoreType.DMA((len(SMALL),)),
            pltpu.SemaphoreType.DMA((40,)),
        ],
        compiler_params=pltpu.CompilerParams(
            collective_id=0, has_side_effects=True, vmem_limit_bytes=60 << 20
        ),
        cost_estimate=pl.CostEstimate(
            flops=2 * POOL * 1024 * D, bytes_accessed=POOL * D * 2, transcendentals=0
        ),
    )(pick_ids, pool, queries)
    gains, own_cover = pl.pallas_call(
        choose,
        name="choose",
        out_shape=(jax.ShapeDtypeStruct((8, TILE), f32), jax.ShapeDtypeStruct((1, TILE), f32)),
        in_specs=[vmem, vmem, vmem],
        out_specs=(vmem, vmem),
    )(part, cover, cand_ids.reshape(8, TILE))
    return gains.reshape(-1), own_cover.reshape(-1)


def solution(mesh):
    in_specs = (
        P(("cand", "query"), None),
        P(("cand", "query")),
        P(("cand", "query")),
        P("query", None),
    )
    out_specs = (P(("cand", "query")), P("query"))
    return jax.shard_map(
        on_device, mesh=mesh, in_specs=in_specs, out_specs=out_specs, check_vma=False
    )
```

```python
import jax
import jax.numpy as jnp
from jax import lax
from jax.experimental import pallas as pl
from jax.experimental.pallas import tpu as pltpu
from jax.sharding import PartitionSpec as P

MESH = pl.DeviceIdType.MESH
D = 4096
TILE = 128
BLOCK = 128
POOL = 1280
SCALE = 1.0 / 64.0
SMALL = ["", "p", "cx", "cz", "cq"]
OWN, X, YP, YM, XP, XM, Y2, X2 = range(8)
DELTA = {X: (0, 1), YP: (1, 0), YM: (3, 0), XP: (1, 1), XM: (3, 1), Y2: (2, 0), X2: (2, 1)}


def where_am_i():
    cand, query = lax.axis_index("cand"), lax.axis_index("query")
    core = lax.rem(cand, 2)
    x = lax.rem(lax.div(cand, 2), 2) * 2 + lax.rem(query, 2)
    return x, lax.div(query, 2), lax.div(cand, 4), core


def device(x, y, z, core):
    return ((z * 2 + lax.div(x, 2)) * 2 + core, y * 2 + lax.rem(x, 2))


def dot(a, b):
    return lax.dot_general(a, b, (((1,), (1,)), ((), ())), preferred_element_type=jnp.float32)


def gather_and_score(
    pick_ref, pool_ref, q_ref, part_ref, cover_ref,
    allq, pool, scores, pick_f32, pick_buf, pick_rows, cover_x, cover_z, cover_q, columns,
    local_sem, send_sem, recv_sem,
):
    x, y, z, core = where_am_i()
    odd = lax.rem(z, 2)
    x_pair = x + 1 - 2 * lax.rem(x, 2)

    def step(v, by, size):
        return lax.rem(v + by + size, size)

    target = {
        "x+": device(step(x, 1, 4), y, z, core),
        "x-": device(step(x, -1, 4), y, z, core),
        "y+": device(x, step(y, 1, 4), z, core),
        "y-": device(x, step(y, -1, 4), z, core),
        "z+": device(x, y, step(z, 1, 8), core),
        "z-": device(x, y, step(z, -1, 8), core),
        "s": device(x, y, z, 1 - core),
    }
    query_group = {
        b: device(x_pair if dx else x, step(y, dy, 4), z, core) for b, (dy, dx) in DELTA.items()
    }
    x_far = step(x, 2, 4)
    four = [device(x_far, y, z, core), device(x, y, z, 1 - core), device(x_far, y, z, 1 - core)]
    column_group = [device(x, y, step(z, d, 8), core) for d in range(1, 8)]

    half_pool = POOL // 2
    pool_copies = [
        pltpu.make_async_copy(
            pool_ref.at[pl.ds(h * half_pool, half_pool)],
            pool.at[pl.ds(h * half_pool, half_pool)],
            local_sem.at[h],
        )
        for h in range(2)
    ]
    own_copy = pltpu.make_async_copy(q_ref, allq.at[pl.ds(0, BLOCK)], local_sem.at[2])
    own_copy.start()
    for c in pool_copies:
        c.start()

    barrier = pltpu.get_barrier_semaphore()
    partners = list(query_group.values()) + four + column_group
    partners += [device(lax.rem(x_pair + 2, 4), y, z, core)]
    for p in partners:
        pl.semaphore_signal(barrier, inc=1, device_id=p, device_id_type=MESH)
    pl.semaphore_wait(barrier, len(partners))

    def pick_col(if_odd, if_even):
        return pl.multiple_of((if_even + odd * (if_odd - if_even)) * TILE, TILE)

    COLS = {
        "c0": (0, 24, 8), "c1": (8, 16, 8), "c2": (16, 8, 8), "cz": (24, 0, 8),
        "c0a": (0, 24, 4), "c0b": (4, 28, 4), "c2a": (16, 8, 4), "c2b": (20, 12, 4), "cza": (24, 0, 4), "czb": (28, 4, 4), "e": (0, 16, 16), "l": (16, 0, 16), "all": (0, 0, 32),
    }

    groups = {}
    sent = [0]

    def send(group, to, src_block, dst_block, cols, rows=(0, 64)):
        if_odd, if_even, tiles = COLS[cols]
        width = pl.ds(pick_col(if_odd, if_even), tiles * TILE)
        first = pl.multiple_of(core * 64 + rows[0], 32)
        src = q_ref if src_block == OWN else allq
        n = groups.setdefault(group, [len(groups), 0, tiles])
        n[1] += rows[1]
        sent[0] += rows[1] // 32 * tiles
        pltpu.make_async_remote_copy(
            src_ref=src.at[pl.ds(pl.multiple_of(src_block * BLOCK + first, 32), rows[1]), width],
            dst_ref=allq.at[pl.ds(pl.multiple_of(dst_block * BLOCK + first, 32), rows[1]), width],
            send_sem=send_sem.at[0],
            recv_sem=recv_sem.at[n[0]],
            device_id=target[to],
            device_id_type=MESH,
        ).start()

    def send_small(group, src, dst, to):
        n = groups.setdefault(group, [len(groups), 0, 1])
        pltpu.make_async_remote_copy(
            src_ref=src, dst_ref=dst, send_sem=send_sem.at[SMALL.index(group)], recv_sem=recv_sem.at[n[0]],
            device_id=to, device_id_type=MESH,
        ).start()

    def got(*names):
        for group in names:
            n, rows, tiles = groups[group]
            ref = allq.at[pl.ds(0, rows), pl.ds(0, tiles * TILE)]
            pltpu.make_async_copy(ref, ref, recv_sem.at[n]).wait()

    def all_small(group, ref, rows):
        ref = ref.at[pl.ds(0, rows)]
        return pltpu.make_async_copy(ref, ref, recv_sem.at[groups[group][0]])

    def along_z(group, block, cols):
        send(group, "z+", block, block, cols, (0, 32))
        send(group, "z-", block, block, cols, (32, 32))

    def share(group, part, *blocks):
        for block in blocks:
            send(group, "s", block, block, part)

    def score(step):
        in_pair = lax.rem(step + lax.div(step, 2) * (1 - lax.div(step, 4)), 2)
        pair = 2 * lax.div(step, 4) + in_pair
        rows = pl.ds(pl.multiple_of(pair * 2 * BLOCK, 2 * BLOCK), 2 * BLOCK)
        late = lax.div(lax.rem(step, 4), 2)
        width = pl.ds(pl.multiple_of(lax.rem(late + 1 + odd, 2) * (D // 2), D // 2), D // 2)
        scores[rows, :] = scores[rows, :] + dot(allq[rows, width], pool[:, width])

    def gain(first, groups, carry):
        def body(g, carry):
            summed, highest = carry
            r = pl.ds(pl.multiple_of(first + g * 8, 8), 8)
            s = scores[r, :]
            c = jnp.concatenate([columns[r, :]] * (POOL // TILE), axis=1)
            return summed + jnp.maximum(s - c, 0.0), jnp.maximum(highest, s)

        return lax.fori_loop(0, groups, body, carry)

    for k in "ab":
        send("Y0" + k, "y-", OWN, YP, "c0" + k)
        send("Y0" + k, "y+", OWN, YM, "c0" + k)
    send("X", "x+", OWN, X, "c0")
    send("X", "x-", OWN, X, "c1")

    own_copy.wait()
    for c in pool_copies:
        c.wait()
    pick = pick_ref[0]
    near = pool.reshape(POOL // 16, 16, D)[lax.div(pick, 16)].astype(jnp.float32)
    is_pick = lax.broadcasted_iota(jnp.int32, (16, D), 0) == lax.rem(pick, 16)
    row = jnp.sum(jnp.where(is_pick, near, 0.0), axis=0, keepdims=True)
    for i in range(D // TILE):
        pick_f32[pl.ds(i, 1), :] = row[:, i * TILE : (i + 1) * TILE]
    pick_buf[pl.ds(0, 32), :] = pick_f32[pl.ds(0, 32), :].astype(jnp.bfloat16)
    back = {X: X, YP: YM, YM: YP, XP: XM, XM: XP, Y2: Y2, X2: X2}
    for b, to in query_group.items():
        send_small("p", pick_buf.at[pl.ds(0, 32)], pick_buf.at[pl.ds(back[b] * 32, 32)], to)

    for k in "12":
        send("Y" + k, "y-", OWN, YP, "c" + k)
        send("Y" + k, "y+", OWN, YM, "c" + k)

    def clear(g, _):
        scores[pl.ds(pl.multiple_of(g * 8, 8), 8), :] = jnp.zeros((8, POOL), jnp.float32)
        return 0

    lax.fori_loop(0, 8 * BLOCK // 8, clear, 0)

    def before_0():
        for k in "ab":
            got("Y0" + k)
            send("XP0" + k, "x+", YP, XP, "c0" + k)
            send("XP0" + k, "x-", YM, XM, "c0" + k)
        along_z("zY", YP, "c0")
        along_z("zY", YM, "c0")
        got("X")
        share("sXe", "e", X)
        along_z("zX", X, "e")
        all_small("p", pick_buf, 7 * 32).wait()
        pick_f32[...] = pick_buf[...].astype(jnp.float32)
        for i in range(D // TILE):
            pick_rows[:, pl.ds(i * TILE, TILE)] = pick_f32[pl.ds(i, 8, stride=32), :]
        eight = pick_rows[...].astype(jnp.bfloat16)
        sims = dot(jnp.concatenate([eight, eight], axis=0), allq[pl.ds(0, BLOCK), :])
        cover_x[pl.ds(0, 8), :] = jnp.broadcast_to(jnp.max(sims, axis=0, keepdims=True), (8, TILE))
        for i, to in enumerate(four):
            send_small("cx", cover_x.at[pl.ds(0, 8)], cover_x.at[pl.ds(8 + 8 * i, 8)], to)
        got("Y1")
        send("XP1", "x+", YP, XP, "c1")
        send("XP1", "x-", YM, XM, "c1")
        share("sYe", "e", YP, YM)
        send("Y2e", "y-", YP, Y2, "c0")
        send("Y2e", "y+", YM, Y2, "c1")
        got("sXe")

    def before_1():
        got("zY")
        send("XPz", "x+", YP, XP, "cz")
        send("XPz", "x-", YM, XM, "cz")
        got("Y2")
        send("XP2", "x+", YP, XP, "c2")
        send("XP2", "x-", YM, XM, "c2")
        send("Y2l", "y-", YP, Y2, "cz")
        send("Y2l", "y+", YM, Y2, "c2")
        share("sYl", "l", YP, YM)
        got("sYe")

    def before_2():
        got("XP0a", "XP0b", "XP1")
        send("X2e", "y-", XP, X2, "c0")
        send("X2e", "y+", XM, X2, "c1")
        share("sXPe", "e", XP, XM)
        got("zX")
        share("sXl", "l", X)
        got("Y2e")
        share("sY2e", "e", Y2)
        all_small("cx", cover_x, 24).wait()
        best = jnp.maximum(
            jnp.maximum(cover_x[pl.ds(0, 8), :], cover_x[pl.ds(8, 8), :]),
            jnp.maximum(cover_x[pl.ds(16, 8), :], cover_x[pl.ds(24, 8), :]),
        )
        cover_z[pl.ds(0, 8), :] = best
        for i, to in enumerate(column_group):
            send_small("cz", cover_z.at[pl.ds(0, 8)], cover_z.at[pl.ds(8 + 8 * i, 8)], to)
        got("sYl")

    def before_3():
        got("sXl")

    def before_4():
        got("Y2l")
        send("X2l", "x+", Y2, X2, "c2a")
        send("X2l", "x-", Y2, X2, "c2b")
        got("XPz")
        send("X2l", "y-", XP, X2, "cza")
        send("X2l", "y+", XM, X2, "czb")
        share("sY2l", "l", Y2)
        got("sXPe")

    def before_5():
        all_small("cz", cover_z, 56).wait()
        best = cover_z[pl.ds(0, 8), :]
        for i in range(7):
            best = jnp.maximum(best, cover_z[pl.ds(8 + 8 * i, 8), :])
        cover_q[pl.ds(0, 8), :] = best
        cover_ref[...] = best
        for b, to in query_group.items():
            send_small("cq", cover_q.at[pl.ds(0, 8)], cover_q.at[pl.ds(back[b] * 8, 8)], to)
        got("XP2")
        share("sXPl", "l", XP, XM)
        got("X2e")
        share("sX2e", "e", X2)
        got("sY2e", "sX2e")

    def before_6():
        got("X2l")
        share("sX2l", "l", X2)
        got("sXPl")

    def before_7():
        all_small("cq", cover_q, 56).wait()
        rows = jnp.concatenate(
            [cover_q[pl.ds(8 * b, 1), :] for b in range(8)] + [jnp.zeros((TILE - 8, TILE), jnp.float32)], axis=0
        )
        turned = rows.T
        for b in range(8):
            columns[pl.ds(b * BLOCK, BLOCK), :] = jnp.broadcast_to(turned[:, b : b + 1], (BLOCK, TILE))
        start = (jnp.zeros((8, POOL), jnp.float32), jnp.full((8, POOL), -jnp.inf, jnp.float32))
        summed, highest = gain(0, 6 * BLOCK // 8, start)
        part_ref[pl.ds(0, 8), :] = summed
        part_ref[pl.ds(8, 8), :] = highest
        got("sY2l", "sX2l")

    before = [before_0, before_1, before_2, before_3, before_4, before_5, before_6, before_7]

    def one_step(step, _):
        for k, segment in enumerate(before):
            pl.when(step == k)(segment)
        score(step)
        return 0

    lax.fori_loop(0, len(before), one_step, 0)

    summed, highest = gain(6 * BLOCK, 2 * BLOCK // 8, (part_ref[pl.ds(0, 8), :], part_ref[pl.ds(8, 8), :]))
    part_ref[pl.ds(0, 8), :] = summed
    part_ref[pl.ds(8, 8), :] = highest

    wide, rest = divmod(sent[0], 8 * BLOCK // 32)
    for n, tiles in ((8 * BLOCK, wide), (rest * 32, 1)):
        if n and tiles:
            ref = allq.at[pl.ds(0, n), pl.ds(0, tiles * TILE)]
            pltpu.make_async_copy(ref, ref, send_sem.at[0]).wait()
    for group, buffer, rows in (("p", pick_buf, 224), ("cx", cover_x, 24), ("cz", cover_z, 56), ("cq", cover_q, 56)):
        ref = buffer.at[pl.ds(0, rows)]
        pltpu.make_async_copy(ref, ref, send_sem.at[SMALL.index(group)]).wait()


def choose(part_ref, cover_ref, ids_ref, gains_ref, out_cover_ref):
    summed = jnp.sum(part_ref[pl.ds(0, 8), :], axis=0, keepdims=True)
    highest = jnp.max(part_ref[pl.ds(8, 8), :], axis=0, keepdims=True)
    gain = summed * SCALE + 1.0 * (highest * SCALE)
    ids = ids_ref[...]
    lane, group = jnp.bitwise_and(ids, TILE - 1), jnp.right_shift(ids, 7)
    out = jnp.zeros(ids.shape, jnp.float32)
    for k in range(POOL // TILE):
        row = jnp.broadcast_to(gain[:, k * TILE : (k + 1) * TILE], ids.shape)
        out = jnp.where(group == k, jnp.take_along_axis(row, lane, axis=1, mode="promise_in_bounds"), out)
    gains_ref[...] = out
    out_cover_ref[...] = cover_ref[pl.ds(0, 1), :] * SCALE


def on_device(pool, cand_ids, pick_ids, queries):
    f32, bf16 = jnp.float32, jnp.bfloat16
    vmem = pl.BlockSpec(memory_space=pltpu.VMEM)
    part, cover = pl.pallas_call(
        gather_and_score,
        name="gather_and_score",
        out_shape=(jax.ShapeDtypeStruct((16, POOL), f32), jax.ShapeDtypeStruct((8, TILE), f32)),
        in_specs=[
            pl.BlockSpec(memory_space=pltpu.SMEM),
            pl.BlockSpec(memory_space=pl.ANY),
            pl.BlockSpec(memory_space=pl.ANY),
        ],
        out_specs=(vmem, vmem),
        scratch_shapes=[
            pltpu.VMEM((8 * BLOCK, D), bf16),
            pltpu.VMEM((POOL, D), bf16),
            pltpu.VMEM((8 * BLOCK, POOL), f32),
            pltpu.VMEM((256, TILE), f32),
            pltpu.VMEM((256, TILE), bf16),
            pltpu.VMEM((8, D), f32),
            pltpu.VMEM((32, TILE), f32),
            pltpu.VMEM((64, TILE), f32),
            pltpu.VMEM((64, TILE), f32),
            pltpu.VMEM((8 * BLOCK, TILE), f32),
            pltpu.SemaphoreType.DMA((3,)),
            pltpu.SemaphoreType.DMA((len(SMALL),)),
            pltpu.SemaphoreType.DMA((40,)),
        ],
        compiler_params=pltpu.CompilerParams(
            collective_id=0, has_side_effects=True, vmem_limit_bytes=60 << 20
        ),
        cost_estimate=pl.CostEstimate(
            flops=2 * POOL * 1024 * D, bytes_accessed=POOL * D * 2, transcendentals=0
        ),
    )(pick_ids, pool, queries)
    gains, own_cover = pl.pallas_call(
        choose,
        name="choose",
        out_shape=(jax.ShapeDtypeStruct((8, TILE), f32), jax.ShapeDtypeStruct((1, TILE), f32)),
        in_specs=[vmem, vmem, vmem],
        out_specs=(vmem, vmem),
    )(part, cover, cand_ids.reshape(8, TILE))
    return gains.reshape(-1), own_cover.reshape(-1)


def solution(mesh):
    in_specs = (
        P(("cand", "query"), None),
        P(("cand", "query")),
        P(("cand", "query")),
        P("query", None),
    )
    out_specs = (P(("cand", "query")), P("query"))
    return jax.shard_map(
        on_device, mesh=mesh, in_specs=in_specs, out_specs=out_specs, check_vma=False
    )
```
